32 devices in a mesh: grp: 2 (over x), ctx: 16 (over z, y, core).
Axes of the slice: x: 2, y: 2, z: 4, core: 2. Of those that a mesh axis runs over, the one named last changes fastest.
Arguments:
- cotangent: bfloat16 [12288, 2048], P(('grp', 'ctx')), parts along dimension 0, may hold values from -6 to 6
- vis_count: int32 [32], P('grp'), parts along dimension 0, may hold values from 0 to 384, as said below
- vis_pos: int32 [12288], P(('grp', 'ctx')), parts along dimension 0, may hold values from 0 to 383, as said below
- patch_owner: int32 [6144], P('grp'), parts along dimension 0, may hold values from 0 to 15, as said below
- pre_act: bfloat16 [6144, 2304], P(('grp', 'ctx')), parts along dimension 0, may hold values from -6 to 6
- proj_weight: bfloat16 [2304, 2048], P('ctx'), may hold values from -0.125 to 0.125
Outputs:
- pre_act_grad: bfloat16 [6144, 2304], P(('grp', 'ctx')), parts along dimension 0
- hidden_bias_grad: float32 [4608], P('grp'), parts along dimension 0
- out_bias_grad: float32 [4096], P('grp'), parts along dimension 0
The draws below stay inside these ranges and needn't reach their ends.
There are 2 independent parts, one for each index of `grp`. The reference program is written for one: setup_inputs(seed, part) draws one part's arguments, and reference() takes and returns one part's arrays. A program takes and returns all parts, laid end to end along the dimension named above; an argument that names none is the same for every part. Nothing has to cross between parts.
Inputs may be any that keep to these rules, and one draw needn't show every extreme that they name: `vis_count`: each entry is 16 times a whole number; the entries sum to 3072; the largest is 384. `vis_pos`: for each shard s the 384 entries from s * 384 are a permutation of the local positions: first the vis_count[s] visual positions in ascending order, then the others in ascending order. `patch_owner`: entry v is the context index of the device that holds visual token v; each aligned block of 16 entries names every index once, so every owner holds 192 visual tokens, token v in its row v // 16.
All inputs are finite; a program needn't handle non-finite values.
Results may differ from the reference program's by a relative error of at most 0.001.
Values may be sent and summed in bfloat16 or wider, within the bound.
A program may use at most 128 MiB of HBM per device.

```python
import math
import jax
import jax.numpy as jnp
from jax import lax

C = 2048
H = 2304
TOK_DEV = 384
TOKENS = 6144
VIS_DEV = 192
VIS_TOTAL = 3072
N_CTX = 16


def block_counts_of(key):
    base = jax.random.fold_in(key, 11)
    shuffle_key = jax.random.fold_in(base, 1)
    shift_key = jax.random.fold_in(base, 2)
    half_share = TOK_DEV // N_CTX // 2
    shuffle = jax.random.permutation(shuffle_key, N_CTX)
    shifts = jax.random.randint(shift_key, (N_CTX // 2,), 0, half_share + 1)
    shifts = shifts.at[0].set(half_share)
    larger = (half_share + shifts).astype(jnp.int32)
    smaller = (half_share - shifts).astype(jnp.int32)
    blocks = jnp.zeros((N_CTX,), jnp.int32)
    blocks = blocks.at[shuffle[0::2]].set(larger)
    blocks = blocks.at[shuffle[1::2]].set(smaller)
    return blocks


def draw_vis_count(key, part):
    blocks = block_counts_of(key)
    return (blocks * N_CTX).astype(jnp.int32)


def draw_vis_pos(key, part):
    blocks = block_counts_of(key)
    key = jax.random.fold_in(key, 2)
    counts = blocks * N_CTX
    shard_keys = jax.random.split(key, N_CTX)
    shuffles = jax.vmap(lambda one_key: jax.random.permutation(one_key, TOK_DEV))(shard_keys)
    ranks = jnp.argsort(shuffles, axis=1, stable=True).astype(jnp.int32)
    positions = jnp.arange(TOK_DEV, dtype=jnp.int32)[None, :]
    chosen = ranks < counts[:, None]
    sort_keys = jnp.where(chosen, positions, positions + TOK_DEV)
    ordered = jnp.argsort(sort_keys, axis=1, stable=True).astype(jnp.int32)
    return ordered.reshape(-1)


def draw_patch_owner(key, part):
    key = jax.random.fold_in(key, 3)
    block_keys = jax.random.split(key, VIS_TOTAL // N_CTX)
    owners = jax.vmap(lambda one_key: jax.random.permutation(one_key, N_CTX))(block_keys)
    return owners.reshape(-1).astype(jnp.int32)


def shard_levels(key, shape, shards, low, top_value):
    loudness, own = 1.0, jax.random.fold_in(key, 6)
    for axis_at, parts in shards:
        draws = jnp.exp(jax.random.uniform(jax.random.fold_in(own, axis_at), (parts,), jnp.float32, low / len(shards), top_value / len(shards)))
        loudness = loudness * jnp.repeat(draws, shape[axis_at] // parts).reshape([-1 if axis == axis_at else 1 for axis in range(len(shape))])
    return loudness


def scatter_about(stream_key, extent, deviation, most, cuts=(), kind=jnp.bfloat16):
    values = jax.random.normal(stream_key, extent, jnp.float32) * deviation
    if len(cuts) > 0:
        values = shard_levels(stream_key, extent, cuts, -0.22, 0.18) * values
    return jnp.clip(values, min=-most, max=most).astype(kind)


def setup_inputs(seed: int = 0, part: int = 0) -> dict:
    keys = jax.random.split(jax.random.key(seed), 7)
    own_keys = jax.random.split(jax.random.fold_in(keys[6], part), 7)
    return {
        "cotangent": scatter_about(own_keys[0], (TOKENS, C), 1.0, 6.0, ((0, 16),)),
        "vis_count": draw_vis_count(jax.random.fold_in(jax.random.fold_in(keys[6], part), 71), part),
        "vis_pos": draw_vis_pos(jax.random.fold_in(jax.random.fold_in(keys[6], part), 71), part),
        "patch_owner": draw_patch_owner(jax.random.fold_in(jax.random.fold_in(keys[6], part), 71), part),
        "pre_act": scatter_about(own_keys[4], (VIS_TOTAL, H), 1.0, 6.0, ((0, 16),)),
        "proj_weight": scatter_about(keys[5], (H, C), H ** -0.5, 0.125, ((0, 16),)),
    }


def gelu_tanh(values):
    return jax.nn.gelu(values, approximate=True)

def reference(cotangent, vis_count, vis_pos, patch_owner, pre_act, proj_weight):
    counts = vis_count.astype(jnp.int32)
    starts = (jnp.cumsum(counts) - counts).astype(jnp.int32)
    local_ids = jnp.arange(TOK_DEV, dtype=jnp.int32)
    shard_ids = jnp.arange(N_CTX, dtype=jnp.int32)
    token_ids = starts[:, None] + local_ids[None, :]
    visible = local_ids[None, :] < counts[:, None]
    owners = patch_owner[jnp.minimum(token_ids, VIS_TOTAL - 1)].astype(jnp.int32)
    target = jnp.where(visible, owners * VIS_DEV + token_ids // N_CTX, VIS_TOTAL).astype(jnp.int32)
    source_rows = (shard_ids[:, None] * TOK_DEV + vis_pos.reshape(N_CTX, TOK_DEV)).astype(jnp.int32)
    picked = cotangent[source_rows.reshape(-1)]
    grad_rows = jnp.zeros((VIS_TOTAL, C), jnp.bfloat16).at[target.reshape(-1)].set(picked, mode='drop')
    act_full, pullback = jax.vjp(gelu_tanh, pre_act.astype(jnp.float32))
    act_grad = jnp.dot(grad_rows, proj_weight.T, preferred_element_type=jnp.float32)
    hidden_grad = pullback(act_grad)[0]
    scale = 1.0 / math.sqrt(VIS_TOTAL)
    hidden_bias_grad = lax.optimization_barrier(jnp.sum(hidden_grad, axis=0)) * scale
    out_bias_grad = lax.optimization_barrier(jnp.sum(grad_rows.astype(jnp.float32), axis=0)) * scale
    return (hidden_grad.astype(jnp.bfloat16), hidden_bias_grad, out_bias_grad)
```

```python
import functools
import math

import jax
import jax.numpy as jnp
from jax import lax
from jax.experimental import pallas as pl
from jax.experimental.pallas import tpu as pltpu
from jax.sharding import PartitionSpec as P

QUARTERS = 4
MESH = pl.DeviceIdType.MESH


def gelu_slope(x):
    k = math.sqrt(2.0 / math.pi)
    square = x * x
    t = jnp.tanh(x * (k + (k * 0.044715) * square))
    return 0.5 * (1.0 + t) + (0.5 * x) * ((1.0 - t * t) * (k + (3.0 * 0.044715 * k) * square))


def kernel(
    grp_size,
    ctx_size,
    z_size,
    y_size,
    scale,
    target_ref,
    slot_ref,
    pos_ref,
    cot_ref,
    pre_ref,
    w_ref,
    out_ref,
    hidden_ref,
    bias_ref,
    w_all,
    outgoing,
    received,
    rows,
    bias_parts,
    hidden_parts,
    w_recv,
    z_send,
    y_send,
    x_send,
    s_send,
    row_send,
    row_recv,
    bias_send,
    bias_recv,
    hidden_send,
    hidden_recv,
):
    grp = lax.axis_index("grp")
    me = lax.axis_index("ctx")
    core = lax.rem(me, 2)
    chip = me // 2
    y = lax.rem(chip, y_size)
    z = chip // y_size
    chips = z_size * y_size
    shared = grp_size % 2 == 0
    own_quarters = QUARTERS // 2 if shared else QUARTERS
    half = lax.rem(grp, 2) if shared else 0
    first_quarter = half * own_quarters
    other_quarter = (1 - half) * own_quarters
    width = w_all.shape[3]
    tok_rows = cot_ref.shape[0]
    per_peer = tok_rows // ctx_size

    def index(z_at, y_at, core_at):
        return (z_at * y_size + y_at) * 2 + core_at

    sibling = {"ctx": index(z, y, 1 - core)}
    y_peer = {"ctx": index(z, y_size - 1 - y, core)}
    z_up = {"ctx": index(jnp.minimum(z + 1, z_size - 1), y, core)}
    z_down = {"ctx": index(jnp.maximum(z - 1, 0), y, core)}
    x_peer = {"grp": grp + 1 - 2 * lax.rem(grp, 2)}

    barrier = pltpu.get_barrier_semaphore()

    def greet(step, carry):
        pl.semaphore_signal(
            barrier, inc=1, device_id={"ctx": lax.rem(me + step, ctx_size)}, device_id_type=MESH
        )
        return carry

    lax.fori_loop(1, ctx_size, greet, 0)
    if shared:
        pl.semaphore_signal(barrier, inc=1, device_id=x_peer, device_id_type=MESH)
    for quarter in range(QUARTERS):
        w_all[quarter, me] = w_ref[:, quarter * width : (quarter + 1) * width]
    pl.semaphore_wait(barrier, ctx_size if shared else ctx_size - 1)

    def piece(quarter, origin, sem, device):
        return pltpu.make_async_remote_copy(
            src_ref=w_all.at[quarter, origin],
            dst_ref=w_all.at[quarter, origin],
            send_sem=sem,
            recv_sem=w_recv.at[quarter, origin],
            device_id=device,
            device_id_type=MESH,
        )

    def up(n, z_at):
        return piece(first_quarter + n, index(z_at, y, core), z_send.at[0, n, z_at], z_up)

    def down(n, z_at):
        return piece(first_quarter + n, index(z_at, y, core), z_send.at[1, n, z_at], z_down)

    def across(n, z_at):
        return piece(first_quarter + n, index(z_at, y, core), y_send.at[n, z_at], y_peer)

    def over(n, z_at, y_at):
        return piece(
            first_quarter + n,
            index(z_at, y_at, core),
            x_send.at[n, z_at * y_size + y_at],
            x_peer,
        )

    def beside(quarter, z_at, y_at):
        return piece(
            quarter, index(z_at, y_at, core), s_send.at[quarter, z_at * y_size + y_at], sibling
        )

    def arrived(quarter, origin):
        piece(quarter, origin, s_send.at[0, 0], sibling).wait_recv()

    for n in range(own_quarters):

        @pl.when(z < z_size - 1)
        def _():
            up(n, z).start()

        @pl.when(z > 0)
        def _():
            down(n, z).start()

        if y_size > 1:
            across(n, z).start()
    for quarter in range(QUARTERS):
        beside(quarter, z, y).start()

    slots = lax.broadcasted_iota(jnp.int32, (tok_rows, tok_rows), 0)
    to_slot = jnp.where(slots == target_ref[...], 1.0, 0.0).astype(jnp.bfloat16)
    to_pos = jnp.where(slots == pos_ref[...], 1.0, 0.0).astype(jnp.bfloat16)
    pick = lax.dot_general(
        to_slot, to_pos, (((1,), (1,)), ((), ())), preferred_element_type=jnp.float32
    ).astype(jnp.bfloat16)
    step_width = 512
    for at in range(0, cot_ref.shape[1], step_width):
        cols = slice(at, at + step_width)
        packed = jnp.dot(pick, cot_ref[:, cols], preferred_element_type=jnp.float32)
        outgoing[:, :, cols] = packed.astype(jnp.bfloat16).reshape(ctx_size, per_peer, step_width)
        bias_parts[me, :, cols] = jnp.sum(packed, axis=0, keepdims=True)

    def row_copy(step):
        peer = lax.rem(me + step, ctx_size)
        return pltpu.make_async_remote_copy(
            src_ref=outgoing.at[peer],
            dst_ref=received.at[me],
            send_sem=row_send.at[peer],
            recv_sem=row_recv.at[me],
            device_id={"ctx": peer},
            device_id_type=MESH,
        )

    def row_arrival(step):
        peer = lax.rem(me + step, ctx_size)
        return pltpu.make_async_remote_copy(
            src_ref=outgoing.at[peer],
            dst_ref=received.at[peer],
            send_sem=row_send.at[peer],
            recv_sem=row_recv.at[peer],
            device_id={"ctx": peer},
            device_id_type=MESH,
        )

    def part_copy(parts, send, recv, step, arrival):
        peer = lax.rem(me + step, ctx_size)
        slot = peer if arrival else me
        return pltpu.make_async_remote_copy(
            src_ref=parts.at[slot],
            dst_ref=parts.at[slot],
            send_sem=send.at[peer],
            recv_sem=recv.at[slot],
            device_id={"ctx": peer},
            device_id_type=MESH,
        )

    def each_peer(body):
        def run(step, carry):
            body(step)
            return carry

        lax.fori_loop(1, ctx_size, run, 0)

    def send_rows(step):
        row_copy(step).start()
        part_copy(bias_parts, bias_send, bias_recv, step, False).start()

    each_peer(send_rows)
    received[me] = outgoing[me]

    def pass_z(z_at, rising):
        for n in range(own_quarters):
            arrived(first_quarter + n, index(z_at, y, core))
            if rising:

                @pl.when(z < z_size - 1)
                def _():
                    up(n, z_at).start()

            else:

                @pl.when(z > 0)
                def _():
                    down(n, z_at).start()

            if y_size > 1:
                across(n, z_at).start()
            if shared:
                over(n, z_at, y).start()
            beside(first_quarter + n, z_at, y).start()

    def pass_y(z_at):
        for n in range(own_quarters):
            arrived(first_quarter + n, index(z_at, y_size - 1 - y, core))
            if shared:
                over(n, z_at, y_size - 1 - y).start()
            beside(first_quarter + n, z_at, y_size - 1 - y).start()

    def pass_x(z_at, y_at):
        for n in range(own_quarters):
            arrived(other_quarter + n, index(z_at, y_at, core))
            beside(other_quarter + n, z_at, y_at).start()

    def at_distance(d, body):
        @pl.when((d >= 0) & (z - d >= 0))
        def _():
            body(z - d, True)

        @pl.when((d > 0) & (z + d < z_size))
        def _():
            body(z + d, False)

    def forward(t, carry):
        @pl.when((t > 0) & (t < z_size))
        def _():
            at_distance(t, pass_z)

        if y_size > 1:

            @pl.when(t - 1 < z_size)
            def _():
                at_distance(t - 1, lambda z_at, rising: pass_y(z_at))

        if shared:

            def both(z_at, rising):
                @pl.when(z_at != z)
                def _():
                    pass_x(z_at, y)

                if y_size > 1:
                    pass_x(z_at, y_size - 1 - y)

            @pl.when(t - 2 < z_size)
            def _():
                at_distance(t - 2, both)

        return carry

    lax.fori_loop(1, z_size + 2, forward, 0)

    each_peer(lambda step: row_arrival(step).wait_recv())
    owned = rows.shape[0]
    slot_ids = lax.broadcasted_iota(jnp.int32, (owned, tok_rows), 0)
    place = jnp.where(slot_ids == slot_ref[...], 1.0, 0.0).astype(jnp.bfloat16)
    for at in range(0, cot_ref.shape[1], step_width):
        cols = slice(at, at + step_width)
        landed = received[:, :, cols].reshape(tok_rows, step_width)
        rows[:, cols] = jnp.dot(place, landed, preferred_element_type=jnp.float32).astype(
            jnp.bfloat16
        )

    def side(chip_at, carry):
        for quarter in range(QUARTERS):
            arrived(quarter, chip_at * 2 + 1 - core)
        return carry

    lax.fori_loop(0, chips, side, 0)

    group = ctx_size // 2
    units = group * w_all.shape[2]

    def multiply(at, carry):
        total = jnp.zeros((owned, units), jnp.float32)
        for quarter in range(QUARTERS):
            block = w_all[quarter, pl.ds(at * group, group)].reshape(units, width)
            total += lax.dot_general(
                rows[:, quarter * width : (quarter + 1) * width],
                block,
                (((1,), (1,)), ((), ())),
                preferred_element_type=jnp.float32,
            )
        cols = pl.ds(pl.multiple_of(at * units, 128), units)
        grad = total * gelu_slope(pre_ref[:, cols].astype(jnp.float32))
        out_ref[:, cols] = grad.astype(jnp.bfloat16)
        hidden_parts[me, :, cols] = jnp.sum(grad, axis=0, keepdims=True)
        return carry

    lax.fori_loop(0, 2, multiply, 0)
    each_peer(
        lambda step: part_copy(hidden_parts, hidden_send, hidden_recv, step, False).start()
    )

    each_peer(lambda step: part_copy(bias_parts, bias_send, bias_recv, step, True).wait_recv())
    bias_ref[...] = jnp.sum(bias_parts[...], axis=0) * scale

    def sent_z(z_at, carry):
        for n in range(own_quarters):

            @pl.when((z < z_size - 1) & (z_at <= z))
            def _():
                up(n, z_at).wait_send()

            @pl.when((z > 0) & (z_at >= z))
            def _():
                down(n, z_at).wait_send()

            if y_size > 1:
                across(n, z_at).wait_send()
        return carry

    lax.fori_loop(0, z_size, sent_z, 0)

    def sent_chip(chip_at, carry):
        z_at = chip_at // y_size
        y_at = lax.rem(chip_at, y_size)
        if shared:

            @pl.when(chip_at != chip)
            def _():
                for n in range(own_quarters):
                    over(n, z_at, y_at).wait_send()

        for quarter in range(QUARTERS):
            beside(quarter, z_at, y_at).wait_send()
        return carry

    lax.fori_loop(0, chips, sent_chip, 0)

    def sent_rows(step):
        row_copy(step).wait_send()
        part_copy(bias_parts, bias_send, bias_recv, step, False).wait_send()

    each_peer(sent_rows)
    each_peer(
        lambda step: part_copy(hidden_parts, hidden_send, hidden_recv, step, True).wait_recv()
    )
    hidden_ref[...] = jnp.sum(hidden_parts[...], axis=0) * scale
    each_peer(
        lambda step: part_copy(hidden_parts, hidden_send, hidden_recv, step, False).wait_send()
    )


def per_device(grp_size, cotangent, vis_count, vis_pos, patch_owner, pre_act, proj_weight):
    ctx_size = lax.axis_size("ctx")
    me = lax.axis_index("ctx")
    tok_rows, row_width = cotangent.shape
    per_peer = tok_rows // ctx_size
    owned, hidden = pre_act.shape
    units, _ = proj_weight.shape
    chips = ctx_size // 2
    y_size = 2 if chips == 8 else 1
    z_size = chips // y_size
    own_quarters = QUARTERS // 2 if grp_size % 2 == 0 else QUARTERS
    width = row_width // QUARTERS

    blocks = vis_count // ctx_size
    peers = jnp.arange(ctx_size, dtype=jnp.int32)
    first = jnp.sum(jnp.where(peers[None, :] < peers[:, None], blocks[None, :], 0), axis=1)
    my_first = jnp.sum(jnp.where(peers < me, blocks, 0))
    my_blocks = jnp.sum(jnp.where(peers == me, blocks, 0))
    padded = jnp.concatenate([patch_owner, jnp.zeros((tok_rows,), jnp.int32)])
    owner = lax.dynamic_slice_in_dim(padded, my_first * ctx_size, tok_rows, 0)
    block_at = jnp.arange(tok_rows, dtype=jnp.int32) // ctx_size
    target = jnp.where(block_at < my_blocks, owner * per_peer + block_at, -1)
    nth = jnp.arange(per_peer, dtype=jnp.int32)
    slot = jnp.where(nth[None, :] < blocks[:, None], first[:, None] + nth[None, :], -1)

    vmem = pl.BlockSpec(memory_space=pltpu.VMEM)
    dma = pltpu.SemaphoreType.DMA
    pre_act_grad, hidden_sum, out_sum = pl.pallas_call(
        functools.partial(
            kernel, grp_size, ctx_size, z_size, y_size, 1.0 / math.sqrt(owned * ctx_size)
        ),
        out_shape=(
            jax.ShapeDtypeStruct((owned, hidden), jnp.bfloat16),
            jax.ShapeDtypeStruct((1, hidden), jnp.float32),
            jax.ShapeDtypeStruct((1, row_width), jnp.float32),
        ),
        in_specs=[vmem] * 6,
        out_specs=(vmem, vmem, vmem),
        scratch_shapes=[
            pltpu.VMEM((QUARTERS, ctx_size, units, width), jnp.bfloat16),
            pltpu.VMEM((ctx_size, per_peer, row_width), jnp.bfloat16),
            pltpu.VMEM((ctx_size, per_peer, row_width), jnp.bfloat16),
            pltpu.VMEM((owned, row_width), jnp.bfloat16),
            pltpu.VMEM((ctx_size, 1, row_width), jnp.float32),
            pltpu.VMEM((ctx_size, 1, hidden), jnp.float32),
            dma((QUARTERS, ctx_size)),
            dma((2, own_quarters, z_size)),
            dma((own_quarters, z_size)),
            dma((own_quarters, chips)),
            dma((QUARTERS, chips)),
            dma((ctx_size,)),
            dma((ctx_size,)),
            dma((ctx_size,)),
            dma((ctx_size,)),
            dma((ctx_size,)),
            dma((ctx_size,)),
        ],
        compiler_params=pltpu.CompilerParams(
            collective_id=0, has_side_effects=True, vmem_limit_bytes=56 * 1024 * 1024
        ),
        cost_estimate=pl.CostEstimate(
            flops=2 * owned * hidden * row_width,
            bytes_accessed=8 * owned * row_width,
            transcendentals=owned * hidden,
        ),
    )(
        target.reshape(1, tok_rows),
        slot.reshape(1, tok_rows),
        vis_pos.reshape(1, tok_rows),
        cotangent,
        pre_act,
        proj_weight,
    )
    return (pre_act_grad, hidden_sum.reshape(hidden), out_sum.reshape(row_width))


def solution(mesh):
    return jax.shard_map(
        functools.partial(per_device, mesh.shape["grp"]),
        mesh=mesh,
        in_specs=(
            P(("grp", "ctx"), None),
            P("grp"),
            P(("grp", "ctx")),
            P("grp"),
            P(("grp", "ctx"), None),
            P("ctx", None),
        ),
        out_specs=(P(("grp", "ctx"), None), P("grp"), P("grp")),
        check_vma=False,
    )
```

```python
import functools
import math

import jax
import jax.numpy as jnp
from jax import lax
from jax.experimental import pallas as pl
from jax.experimental.pallas import tpu as pltpu
from jax.sharding import PartitionSpec as P

PIECES = 8
SWAPPED = 4
ROW_FROM = 1
MESH = pl.DeviceIdType.MESH


def gelu_slope(x):
    k = math.sqrt(2.0 / math.pi)
    square = x * x
    t = jnp.tanh(x * (k + (k * 0.044715) * square))
    return 0.5 * (1.0 + t) + (0.5 * x) * ((1.0 - t * t) * (k + (3.0 * 0.044715 * k) * square))


def kernel(
    grp_size,
    ctx_size,
    z_size,
    y_size,
    scale,
    count_ref,
    pos_ref,
    owner_ref,
    cot_hbm,
    pre_hbm,
    w_hbm,
    out_ref,
    hidden_ref,
    bias_ref,
    cot_ref,
    pre_ref,
    w_all,
    outgoing,
    received,
    rows,
    bias_parts,
    hidden_parts,
    load_sem,
    w_recv,
    z_send,
    y_send,
    x_send,
    s_send,
    row_send,
    row_recv,
    bias_send,
    bias_recv,
    hidden_send,
    hidden_recv,
):
    grp = lax.axis_index("grp")
    me = lax.axis_index("ctx")
    core = lax.rem(me, 2)
    chip = me // 2
    y = lax.rem(chip, y_size)
    z = chip // y_size
    chips = z_size * y_size
    shared = grp_size % 2 == 0
    swapped = SWAPPED if shared else 0
    own_pieces = PIECES - swapped
    half = lax.rem(grp, 2) if shared else 0
    width = w_all.shape[3]
    tok_rows = cot_ref.shape[0]
    per_peer = tok_rows // ctx_size

    def own_piece(n):
        return half * swapped + n if n < swapped else swapped + n

    def other_piece(n):
        return (1 - half) * swapped + n

    def index(z_at, y_at, core_at):
        return (z_at * y_size + y_at) * 2 + core_at

    sibling = {"ctx": index(z, y, 1 - core)}
    y_peer = {"ctx": index(z, y_size - 1 - y, core)}
    z_up = {"ctx": index(jnp.minimum(z + 1, z_size - 1), y, core)}
    z_down = {"ctx": index(jnp.maximum(z - 1, 0), y, core)}
    x_peer = {"grp": grp + 1 - 2 * lax.rem(grp, 2)}

    own_shard = [
        pltpu.make_async_copy(
            w_hbm.at[:, pl.ds(at * width, width)], w_all.at[at, me], load_sem.at[at]
        )
        for at in range(PIECES)
    ]
    for load in own_shard:
        load.start()
    barrier = pltpu.get_barrier_semaphore()

    def greet(step, carry):
        pl.semaphore_signal(
            barrier, inc=1, device_id={"ctx": lax.rem(me + step, ctx_size)}, device_id_type=MESH
        )
        return carry

    lax.fori_loop(1, ctx_size, greet, 0)
    if shared:
        pl.semaphore_signal(barrier, inc=1, device_id=x_peer, device_id_type=MESH)
    loads = [pltpu.make_async_copy(cot_hbm, cot_ref, load_sem.at[PIECES])]
    loads += [pltpu.make_async_copy(pre_hbm, pre_ref, load_sem.at[PIECES + 1])]
    for load in loads:
        load.start()
    for load in own_shard:
        load.wait()
    pl.semaphore_wait(barrier, ctx_size if shared else ctx_size - 1)

    def piece(quarter, origin, sem, device):
        return pltpu.make_async_remote_copy(
            src_ref=w_all.at[quarter, origin],
            dst_ref=w_all.at[quarter, origin],
            send_sem=sem,
            recv_sem=w_recv.at[quarter, origin],
            device_id=device,
            device_id_type=MESH,
        )

    def up(n, z_at):
        return piece(own_piece(n), index(z_at, y, core), z_send.at[0, n, z_at], z_up)

    def down(n, z_at):
        return piece(own_piece(n), index(z_at, y, core), z_send.at[1, n, z_at], z_down)

    def across(n, z_at):
        return piece(own_piece(n), index(z_at, y, core), y_send.at[n, z_at], y_peer)

    def over(n, z_at, y_at):
        return piece(
            own_piece(n),
            index(z_at, y_at, core),
            x_send.at[n, z_at * y_size + y_at],
            x_peer,
        )

    def beside(quarter, z_at, y_at):
        return piece(
            quarter, index(z_at, y_at, core), s_send.at[quarter, z_at * y_size + y_at], sibling
        )

    def arrived(quarter, origin):
        piece(quarter, origin, s_send.at[0, 0], sibling).wait_recv()

    for n in range(own_pieces):

        @pl.when(z < z_size - 1)
        def _():
            up(n, z).start()

        @pl.when(z > 0)
        def _():
            down(n, z).start()

        if y_size > 1:
            across(n, z).start()
    for quarter in range(PIECES):
        beside(quarter, z, y).start()

    blocks = lax.div(count_ref[...].reshape(1, ctx_size), ctx_size).astype(jnp.float32)
    peers = lax.broadcasted_iota(jnp.int32, (1, ctx_size), 1)
    my_first = jnp.sum(jnp.where(peers < me, blocks, 0.0), axis=1, keepdims=True)
    my_blocks = jnp.sum(jnp.where(peers == me, blocks, 0.0), axis=1, keepdims=True)
    token = lax.broadcasted_iota(jnp.int32, (1, tok_rows), 1)
    start = (my_first * ctx_size).astype(jnp.int32)
    chunk = math.gcd(owner_ref.shape[0], 1024)
    offset = lax.broadcasted_iota(jnp.int32, (chunk, tok_rows), 0) - lax.broadcasted_iota(
        jnp.int32, (chunk, tok_rows), 1
    )
    owner = jnp.zeros((8, tok_rows), jnp.float32)
    for at in range(0, owner_ref.shape[0], chunk):
        part = owner_ref[at : at + chunk].reshape(1, chunk).astype(jnp.float32)
        part = jnp.broadcast_to(part, (8, chunk)).astype(jnp.bfloat16)
        hit = jnp.where(offset == start - at, 1.0, 0.0).astype(jnp.bfloat16)
        owner += jnp.dot(part, hit, preferred_element_type=jnp.float32)
    nth_block = lax.div(token, ctx_size)
    target = jnp.where(
        nth_block.astype(jnp.float32) < my_blocks,
        owner[0:1].astype(jnp.int32) * per_peer + nth_block,
        -1,
    )

    source = lax.div(token, per_peer)
    nth = (token - source * per_peer).astype(jnp.float32)
    peer_rows = lax.broadcasted_iota(jnp.int32, (ctx_size, tok_rows), 0)
    counts = jnp.broadcast_to(blocks, (8, ctx_size)).astype(jnp.bfloat16)
    before = jnp.where(peer_rows < source, 1.0, 0.0).astype(jnp.bfloat16)
    equal = jnp.where(peer_rows == source, 1.0, 0.0).astype(jnp.bfloat16)
    first = jnp.dot(counts, before, preferred_element_type=jnp.float32)[0:1]
    held = jnp.dot(counts, equal, preferred_element_type=jnp.float32)[0:1]
    slot = jnp.where(nth < held, first + nth, -1.0).astype(jnp.int32)

    for load in loads:
        load.wait()
    slots = lax.broadcasted_iota(jnp.int32, (tok_rows, tok_rows), 0)
    to_slot = jnp.where(slots == target, 1.0, 0.0).astype(jnp.bfloat16)
    to_pos = jnp.where(slots == pos_ref[...].reshape(1, tok_rows), 1.0, 0.0).astype(jnp.bfloat16)
    pick = lax.dot_general(
        to_slot, to_pos, (((1,), (1,)), ((), ())), preferred_element_type=jnp.float32
    ).astype(jnp.bfloat16)
    step_width = 512
    for at in range(0, cot_ref.shape[1], step_width):
        cols = slice(at, at + step_width)
        packed = jnp.dot(pick, cot_ref[:, cols], preferred_element_type=jnp.float32)
        outgoing[:, :, cols] = packed.astype(jnp.bfloat16).reshape(ctx_size, per_peer, step_width)
        bias_parts[me, :, cols] = jnp.sum(packed, axis=0, keepdims=True)

    def row_copy(step):
        peer = lax.rem(me + step, ctx_size)
        return pltpu.make_async_remote_copy(
            src_ref=outgoing.at[peer],
            dst_ref=received.at[me],
            send_sem=row_send.at[peer],
            recv_sem=row_recv.at[me],
            device_id={"ctx": peer},
            device_id_type=MESH,
        )

    def row_arrival(step):
        peer = lax.rem(me + step, ctx_size)
        return pltpu.make_async_remote_copy(
            src_ref=outgoing.at[peer],
            dst_ref=received.at[peer],
            send_sem=row_send.at[peer],
            recv_sem=row_recv.at[peer],
            device_id={"ctx": peer},
            device_id_type=MESH,
        )

    def part_copy(parts, send, recv, step, arrival):
        peer = lax.rem(me + step, ctx_size)
        slot = peer if arrival else me
        return pltpu.make_async_remote_copy(
            src_ref=parts.at[slot],
            dst_ref=parts.at[slot],
            send_sem=send.at[peer],
            recv_sem=recv.at[slot],
            device_id={"ctx": peer},
            device_id_type=MESH,
        )

    def each_peer(body):
        def run(step, carry):
            body(step)
            return carry

        lax.fori_loop(1, ctx_size, run, 0)

    def send_rows(step):
        row_copy(step).start()
        part_copy(bias_parts, bias_send, bias_recv, step, False).start()

    received[me] = outgoing[me]
    batch = -(-(ctx_size - 1) // (z_size + 2 - ROW_FROM))

    def send_batch(t):
        @pl.when(t >= ROW_FROM)
        def _():
            def run(at, carry):
                step = (t - ROW_FROM) * batch + at + 1

                @pl.when(step < ctx_size)
                def _():
                    send_rows(step)

                return carry

            lax.fori_loop(0, batch, run, 0)

    def pass_z(z_at, rising):
        for n in range(own_pieces):
            arrived(own_piece(n), index(z_at, y, core))
            if rising:

                @pl.when(z < z_size - 1)
                def _():
                    up(n, z_at).start()

            else:

                @pl.when(z > 0)
                def _():
                    down(n, z_at).start()

            if y_size > 1:
                across(n, z_at).start()
            if n < swapped:
                over(n, z_at, y).start()
            beside(own_piece(n), z_at, y).start()

    def pass_y(z_at):
        for n in range(own_pieces):
            arrived(own_piece(n), index(z_at, y_size - 1 - y, core))
            if n < swapped:
                over(n, z_at, y_size - 1 - y).start()
            beside(own_piece(n), z_at, y_size - 1 - y).start()

    def pass_x(z_at, y_at):
        for n in range(swapped):
            arrived(other_piece(n), index(z_at, y_at, core))
            beside(other_piece(n), z_at, y_at).start()

    def at_distance(d, body):
        @pl.when((d >= 0) & (z - d >= 0))
        def _():
            body(z - d, True)

        @pl.when((d > 0) & (z + d < z_size))
        def _():
            body(z + d, False)

    def forward(t, carry):
        send_batch(t)
        @pl.when((t > 0) & (t < z_size))
        def _():
            at_distance(t, pass_z)

        if y_size > 1:

            @pl.when(t - 1 < z_size)
            def _():
                at_distance(t - 1, lambda z_at, rising: pass_y(z_at))

        if shared:

            def both(z_at, rising):
                @pl.when(z_at != z)
                def _():
                    pass_x(z_at, y)

                if y_size > 1:
                    pass_x(z_at, y_size - 1 - y)

            @pl.when(t - 2 < z_size)
            def _():
                at_distance(t - 2, both)

        return carry

    lax.fori_loop(1, z_size + 2, forward, 0)

    each_peer(lambda step: row_arrival(step).wait_recv())
    owned = rows.shape[0]
    slot_ids = lax.broadcasted_iota(jnp.int32, (owned, tok_rows), 0)
    place = jnp.where(slot_ids == slot, 1.0, 0.0).astype(jnp.bfloat16)
    for at in range(0, cot_ref.shape[1], step_width):
        cols = slice(at, at + step_width)
        landed = received[:, :, cols].reshape(tok_rows, step_width)
        rows[:, cols] = jnp.dot(place, landed, preferred_element_type=jnp.float32).astype(
            jnp.bfloat16
        )

    def side(chip_at, carry):
        for quarter in range(PIECES):
            arrived(quarter, chip_at * 2 + 1 - core)
        return carry

    lax.fori_loop(0, chips, side, 0)

    group = ctx_size // 2
    units = group * w_all.shape[2]

    def multiply(at, carry):
        total = jnp.zeros((owned, units), jnp.float32)
        for quarter in range(PIECES):
            block = w_all[quarter, pl.ds(at * group, group)].reshape(units, width)
            total += lax.dot_general(
                rows[:, quarter * width : (quarter + 1) * width],
                block,
                (((1,), (1,)), ((), ())),
                preferred_element_type=jnp.float32,
            )
        cols = pl.ds(pl.multiple_of(at * units, 128), units)
        grad = total * gelu_slope(pre_ref[:, cols].astype(jnp.float32))
        out_ref[:, cols] = grad.astype(jnp.bfloat16)
        hidden_parts[me, :, cols] = jnp.sum(grad, axis=0, keepdims=True)
        return carry

    lax.fori_loop(0, 2, multiply, 0)
    each_peer(
        lambda step: part_copy(hidden_parts, hidden_send, hidden_recv, step, False).start()
    )

    each_peer(lambda step: part_copy(bias_parts, bias_send, bias_recv, step, True).wait_recv())
    bias_ref[...] = jnp.sum(bias_parts[...], axis=0) * scale

    def sent_z(z_at, carry):
        for n in range(own_pieces):

            @pl.when((z < z_size - 1) & (z_at <= z))
            def _():
                up(n, z_at).wait_send()

            @pl.when((z > 0) & (z_at >= z))
            def _():
                down(n, z_at).wait_send()

            if y_size > 1:
                across(n, z_at).wait_send()
        return carry

    lax.fori_loop(0, z_size, sent_z, 0)

    def sent_chip(chip_at, carry):
        z_at = chip_at // y_size
        y_at = lax.rem(chip_at, y_size)
        if shared:

            @pl.when(chip_at != chip)
            def _():
                for n in range(swapped):
                    over(n, z_at, y_at).wait_send()

        for quarter in range(PIECES):
            beside(quarter, z_at, y_at).wait_send()
        return carry

    lax.fori_loop(0, chips, sent_chip, 0)

    def sent_rows(step):
        row_copy(step).wait_send()
        part_copy(bias_parts, bias_send, bias_recv, step, False).wait_send()

    each_peer(sent_rows)
    each_peer(
        lambda step: part_copy(hidden_parts, hidden_send, hidden_recv, step, True).wait_recv()
    )
    hidden_ref[...] = jnp.sum(hidden_parts[...], axis=0) * scale
    each_peer(
        lambda step: part_copy(hidden_parts, hidden_send, hidden_recv, step, False).wait_send()
    )


def per_device(grp_size, cotangent, vis_count, vis_pos, patch_owner, pre_act, proj_weight):
    ctx_size = lax.axis_size("ctx")
    tok_rows, row_width = cotangent.shape
    per_peer = tok_rows // ctx_size
    owned, hidden = pre_act.shape
    units, _ = proj_weight.shape
    chips = ctx_size // 2
    y_size = 2 if chips == 8 else 1
    z_size = chips // y_size
    swapped = SWAPPED if grp_size % 2 == 0 else 0
    own_pieces = PIECES - swapped
    width = row_width // PIECES

    vmem = pl.BlockSpec(memory_space=pltpu.VMEM)
    dma = pltpu.SemaphoreType.DMA
    pre_act_grad, hidden_sum, out_sum = pl.pallas_call(
        functools.partial(
            kernel, grp_size, ctx_size, z_size, y_size, 1.0 / math.sqrt(owned * ctx_size)
        ),
        out_shape=(
            jax.ShapeDtypeStruct((owned, hidden), jnp.bfloat16),
            jax.ShapeDtypeStruct((1, hidden), jnp.float32),
            jax.ShapeDtypeStruct((1, row_width), jnp.float32),
        ),
        in_specs=[vmem] * 3 + [pl.BlockSpec(memory_space=pl.ANY)] * 3,
        out_specs=(vmem, vmem, vmem),
        scratch_shapes=[
            pltpu.VMEM((tok_rows, row_width), jnp.bfloat16),
            pltpu.VMEM((owned, hidden), jnp.bfloat16),
            pltpu.VMEM((PIECES, ctx_size, units, width), jnp.bfloat16),
            pltpu.VMEM((ctx_size, per_peer, row_width), jnp.bfloat16),
            pltpu.VMEM((ctx_size, per_peer, row_width), jnp.bfloat16),
            pltpu.VMEM((owned, row_width), jnp.bfloat16),
            pltpu.VMEM((ctx_size, 1, row_width), jnp.float32),
            pltpu.VMEM((ctx_size, 1, hidden), jnp.float32),
            dma((PIECES + 2,)),
            dma((PIECES, ctx_size)),
            dma((2, own_pieces, z_size)),
            dma((own_pieces, z_size)),
            dma((max(swapped, 1), chips)),
            dma((PIECES, chips)),
            dma((ctx_size,)),
            dma((ctx_size,)),
            dma((ctx_size,)),
            dma((ctx_size,)),
            dma((ctx_size,)),
            dma((ctx_size,)),
        ],
        compiler_params=pltpu.CompilerParams(
            collective_id=0, has_side_effects=True, vmem_limit_bytes=56 * 1024 * 1024
        ),
        cost_estimate=pl.CostEstimate(
            flops=2 * owned * hidden * row_width,
            bytes_accessed=8 * owned * row_width,
            transcendentals=owned * hidden,
        ),
    )(
        vis_count,
        vis_pos,
        patch_owner,
        cotangent,
        pre_act,
        proj_weight,
    )
    return (pre_act_grad, hidden_sum.reshape(hidden), out_sum.reshape(row_width))


def solution(mesh):
    return jax.shard_map(
        functools.partial(per_device, mesh.shape["grp"]),
        mesh=mesh,
        in_specs=(
            P(("grp", "ctx"), None),
            P("grp"),
            P(("grp", "ctx")),
            P("grp"),
            P(("grp", "ctx"), None),
            P("ctx", None),
        ),
        out_specs=(P(("grp", "ctx"), None), P("grp"), P("grp")),
        check_vma=False,
    )
```

```python
import functools
import math

import jax
import jax.numpy as jnp
from jax import lax
from jax.experimental import pallas as pl
from jax.experimental.pallas import tpu as pltpu
from jax.sharding import PartitionSpec as P

PIECES = 8
SWAPPED = 4
ROW_FROM = 1
MESH = pl.DeviceIdType.MESH


def gelu_slope(x):
    k = math.sqrt(2.0 / math.pi)
    square = x * x
    t = jnp.tanh(x * (k + (k * 0.044715) * square))
    return 0.5 * (1.0 + t) + (0.5 * x) * ((1.0 - t * t) * (k + (3.0 * 0.044715 * k) * square))


def kernel(
    grp_size,
    ctx_size,
    z_size,
    y_size,
    scale,
    count_ref,
    pos_ref,
    owner_ref,
    cot_hbm,
    pre_hbm,
    w_hbm,
    out_ref,
    hidden_ref,
    bias_ref,
    cot_ref,
    pre_ref,
    w_all,
    outgoing,
    received,
    rows,
    bias_parts,
    hidden_parts,
    load_sem,
    w_recv,
    z_send,
    y_send,
    x_send,
    s_send,
    row_send,
    row_recv,
    bias_send,
    bias_recv,
    hidden_send,
    hidden_recv,
):
    grp = lax.axis_index("grp")
    me = lax.axis_index("ctx")
    core = lax.rem(me, 2)
    chip = me // 2
    y = lax.rem(chip, y_size)
    z = chip // y_size
    chips = z_size * y_size
    shared = grp_size % 2 == 0
    swapped = SWAPPED if shared else 0
    own_pieces = PIECES - swapped
    half = lax.rem(grp, 2) if shared else 0
    width = w_all.shape[3]
    tok_rows = cot_ref.shape[0]
    per_peer = tok_rows // ctx_size

    def own_piece(n):
        return half * swapped + n if n < swapped else swapped + n

    def other_piece(n):
        return (1 - half) * swapped + n

    def index(z_at, y_at, core_at):
        return (z_at * y_size + y_at) * 2 + core_at

    sibling = {"ctx": index(z, y, 1 - core)}
    y_peer = {"ctx": index(z, y_size - 1 - y, core)}
    z_up = {"ctx": index(jnp.minimum(z + 1, z_size - 1), y, core)}
    z_down = {"ctx": index(jnp.maximum(z - 1, 0), y, core)}
    x_peer = {"grp": grp + 1 - 2 * lax.rem(grp, 2)}

    own_shard = [
        pltpu.make_async_copy(
            w_hbm.at[:, pl.ds(at * width, width)], w_all.at[at, me], load_sem.at[at]
        )
        for at in range(PIECES)
    ]
    for load in own_shard:
        load.start()
    barrier = pltpu.get_barrier_semaphore()

    def greet(step, carry):
        pl.semaphore_signal(
            barrier, inc=1, device_id={"ctx": lax.rem(me + step, ctx_size)}, device_id_type=MESH
        )
        return carry

    lax.fori_loop(1, ctx_size, greet, 0)
    if shared:
        pl.semaphore_signal(barrier, inc=1, device_id=x_peer, device_id_type=MESH)
    loads = [pltpu.make_async_copy(cot_hbm, cot_ref, load_sem.at[PIECES])]
    loads += [pltpu.make_async_copy(pre_hbm, pre_ref, load_sem.at[PIECES + 1])]
    for load in loads:
        load.start()
    for load in own_shard:
        load.wait()
    pl.semaphore_wait(barrier, ctx_size if shared else ctx_size - 1)

    def piece(quarter, origin, sem, device):
        return pltpu.make_async_remote_copy(
            src_ref=w_all.at[quarter, origin],
            dst_ref=w_all.at[quarter, origin],
            send_sem=sem,
            recv_sem=w_recv.at[quarter, origin],
            device_id=device,
            device_id_type=MESH,
        )

    def up(n, z_at):
        return piece(own_piece(n), index(z_at, y, core), z_send.at[0, n, z_at], z_up)

    def down(n, z_at):
        return piece(own_piece(n), index(z_at, y, core), z_send.at[1, n, z_at], z_down)

    def across(n, z_at):
        return piece(own_piece(n), index(z_at, y, core), y_send.at[n, z_at], y_peer)

    def over(n, z_at, y_at):
        return piece(
            own_piece(n),
            index(z_at, y_at, core),
            x_send.at[n, z_at * y_size + y_at],
            x_peer,
        )

    def beside(quarter, z_at, y_at):
        return piece(
            quarter, index(z_at, y_at, core), s_send.at[quarter, z_at * y_size + y_at], sibling
        )

    def arrived(quarter, origin):
        piece(quarter, origin, s_send.at[0, 0], sibling).wait_recv()

    for n in range(own_pieces):

        @pl.when(z < z_size - 1)
        def _():
            up(n, z).start()

        @pl.when(z > 0)
        def _():
            down(n, z).start()

        if y_size > 1:
            across(n, z).start()
    for quarter in range(PIECES):
        beside(quarter, z, y).start()

    blocks = lax.div(count_ref[...].reshape(1, ctx_size), ctx_size).astype(jnp.float32)
    peers = lax.broadcasted_iota(jnp.int32, (1, ctx_size), 1)
    my_first = jnp.sum(jnp.where(peers < me, blocks, 0.0), axis=1, keepdims=True)
    my_blocks = jnp.sum(jnp.where(peers == me, blocks, 0.0), axis=1, keepdims=True)
    token = lax.broadcasted_iota(jnp.int32, (1, tok_rows), 1)
    start = (my_first * ctx_size).astype(jnp.int32)
    chunk = math.gcd(owner_ref.shape[0], 1024)
    offset = lax.broadcasted_iota(jnp.int32, (chunk, tok_rows), 0) - lax.broadcasted_iota(
        jnp.int32, (chunk, tok_rows), 1
    )
    owner = jnp.zeros((8, tok_rows), jnp.float32)
    for at in range(0, owner_ref.shape[0], chunk):
        part = owner_ref[at : at + chunk].reshape(1, chunk).astype(jnp.float32)
        part = jnp.broadcast_to(part, (8, chunk)).astype(jnp.bfloat16)
        hit = jnp.where(offset == start - at, 1.0, 0.0).astype(jnp.bfloat16)
        owner += jnp.dot(part, hit, preferred_element_type=jnp.float32)
    nth_block = lax.div(token, ctx_size)
    target = jnp.where(
        nth_block.astype(jnp.float32) < my_blocks,
        owner[0:1].astype(jnp.int32) * per_peer + nth_block,
        -1,
    )

    source = lax.div(token, per_peer)
    nth = (token - source * per_peer).astype(jnp.float32)
    peer_rows = lax.broadcasted_iota(jnp.int32, (ctx_size, tok_rows), 0)
    counts = jnp.broadcast_to(blocks, (8, ctx_size)).astype(jnp.bfloat16)
    before = jnp.where(peer_rows < source, 1.0, 0.0).astype(jnp.bfloat16)
    equal = jnp.where(peer_rows == source, 1.0, 0.0).astype(jnp.bfloat16)
    first = jnp.dot(counts, before, preferred_element_type=jnp.float32)[0:1]
    held = jnp.dot(counts, equal, preferred_element_type=jnp.float32)[0:1]
    slot = jnp.where(nth < held, first + nth, -1.0).astype(jnp.int32)

    for load in loads:
        load.wait()
    slots = lax.broadcasted_iota(jnp.int32, (tok_rows, tok_rows), 0)
    to_slot = jnp.where(slots == target, 1.0, 0.0).astype(jnp.bfloat16)
    to_pos = jnp.where(slots == pos_ref[...].reshape(1, tok_rows), 1.0, 0.0).astype(jnp.bfloat16)
    pick = lax.dot_general(
        to_slot, to_pos, (((1,), (1,)), ((), ())), preferred_element_type=jnp.float32
    ).astype(jnp.bfloat16)
    step_width = 512
    for at in range(0, cot_ref.shape[1], step_width):
        cols = slice(at, at + step_width)
        packed = jnp.dot(pick, cot_ref[:, cols], preferred_element_type=jnp.float32)
        outgoing[:, :, cols] = packed.astype(jnp.bfloat16).reshape(ctx_size, per_peer, step_width)
        bias_parts[me, :, cols] = jnp.sum(packed, axis=0, keepdims=True)

    def row_copy(step):
        peer = lax.rem(me + step, ctx_size)
        return pltpu.make_async_remote_copy(
            src_ref=outgoing.at[peer],
            dst_ref=received.at[me],
            send_sem=row_send.at[peer],
            recv_sem=row_recv.at[me],
            device_id={"ctx": peer},
            device_id_type=MESH,
        )

    def row_arrival(step):
        peer = lax.rem(me + step, ctx_size)
        return pltpu.make_async_remote_copy(
            src_ref=outgoing.at[peer],
            dst_ref=received.at[peer],
            send_sem=row_send.at[peer],
            recv_sem=row_recv.at[peer],
            device_id={"ctx": peer},
            device_id_type=MESH,
        )

    def part_copy(parts, send, recv, step, arrival):
        peer = lax.rem(me + step, ctx_size)
        slot = peer if arrival else me
        return pltpu.make_async_remote_copy(
            src_ref=parts.at[slot],
            dst_ref=parts.at[slot],
            send_sem=send.at[peer],
            recv_sem=recv.at[slot],
            device_id={"ctx": peer},
            device_id_type=MESH,
        )

    def each_peer(body):
        def run(step, carry):
            body(step)
            return carry

        lax.fori_loop(1, ctx_size, run, 0)

    def send_rows(step):
        row_copy(step).start()
        part_copy(bias_parts, bias_send, bias_recv, step, False).start()

    received[me] = outgoing[me]
    turns = own_pieces * (z_size + 1)
    batch = max(-(-(ctx_size - 1) // (turns // 2)), 1)

    def send_batch(t, n):
        if n % 2 == 0:
            first_step = ((t - 1) * -(-own_pieces // 2) + n // 2) * batch + 1
            for at in range(batch):

                @pl.when(first_step + at < ctx_size)
                def _():
                    send_rows(lax.rem((first_step + at) * 7, ctx_size))

    def pass_z(n, z_at, rising):
        arrived(own_piece(n), index(z_at, y, core))
        if rising:

            @pl.when(z < z_size - 1)
            def _():
                up(n, z_at).start()

        else:

            @pl.when(z > 0)
            def _():
                down(n, z_at).start()

        if y_size > 1:
            across(n, z_at).start()
        if n < swapped:
            over(n, z_at, y).start()
        beside(own_piece(n), z_at, y).start()

    def pass_y(n, z_at):
        arrived(own_piece(n), index(z_at, y_size - 1 - y, core))
        if n < swapped:
            over(n, z_at, y_size - 1 - y).start()
        beside(own_piece(n), z_at, y_size - 1 - y).start()

    def pass_x(n, z_at, y_at):
        arrived(other_piece(n), index(z_at, y_at, core))
        beside(other_piece(n), z_at, y_at).start()

    def at_distance(d, body):
        @pl.when((d >= 0) & (z - d >= 0))
        def _():
            body(z - d, True)

        @pl.when((d > 0) & (z + d < z_size))
        def _():
            body(z + d, False)

    def forward_piece(n, t):
        @pl.when(t < z_size)
        def _():
            at_distance(t, lambda z_at, rising: pass_z(n, z_at, rising))

        if y_size > 1:

            @pl.when(t - 1 < z_size)
            def _():
                at_distance(t - 1, lambda z_at, rising: pass_y(n, z_at))

        if n < swapped:

            def both(z_at, rising):
                @pl.when(z_at != z)
                def _():
                    pass_x(n, z_at, y)

                if y_size > 1:
                    pass_x(n, z_at, y_size - 1 - y)

            @pl.when(t - 2 < z_size)
            def _():
                at_distance(t - 2, both)

    def forward(t, carry):
        for n in range(own_pieces):
            send_batch(t, n)
            forward_piece(n, t)
        return carry

    lax.fori_loop(1, z_size + 2, forward, 0)

    each_peer(lambda step: row_arrival(step).wait_recv())
    owned = rows.shape[0]
    slot_ids = lax.broadcasted_iota(jnp.int32, (owned, tok_rows), 0)
    place = jnp.where(slot_ids == slot, 1.0, 0.0).astype(jnp.bfloat16)
    for at in range(0, cot_ref.shape[1], step_width):
        cols = slice(at, at + step_width)
        landed = received[:, :, cols].reshape(tok_rows, step_width)
        rows[:, cols] = jnp.dot(place, landed, preferred_element_type=jnp.float32).astype(
            jnp.bfloat16
        )

    def side(chip_at, carry):
        for quarter in range(PIECES):
            arrived(quarter, chip_at * 2 + 1 - core)
        return carry

    lax.fori_loop(0, chips, side, 0)

    group = ctx_size // 2
    units = group * w_all.shape[2]

    def multiply(at, carry):
        total = jnp.zeros((owned, units), jnp.float32)
        for quarter in range(PIECES):
            block = w_all[quarter, pl.ds(at * group, group)].reshape(units, width)
            total += lax.dot_general(
                rows[:, quarter * width : (quarter + 1) * width],
                block,
                (((1,), (1,)), ((), ())),
                preferred_element_type=jnp.float32,
            )
        cols = pl.ds(pl.multiple_of(at * units, 128), units)
        grad = total * gelu_slope(pre_ref[:, cols].astype(jnp.float32))
        out_ref[:, cols] = grad.astype(jnp.bfloat16)
        hidden_parts[me, :, cols] = jnp.sum(grad, axis=0, keepdims=True)
        return carry

    lax.fori_loop(0, 2, multiply, 0)
    each_peer(
        lambda step: part_copy(hidden_parts, hidden_send, hidden_recv, step, False).start()
    )

    each_peer(lambda step: part_copy(bias_parts, bias_send, bias_recv, step, True).wait_recv())
    bias_ref[...] = (jnp.sum(bias_parts[...], axis=0) * scale).reshape(bias_ref.shape)

    def sent_z(z_at, carry):
        for n in range(own_pieces):

            @pl.when((z < z_size - 1) & (z_at <= z))
            def _():
                up(n, z_at).wait_send()

            @pl.when((z > 0) & (z_at >= z))
            def _():
                down(n, z_at).wait_send()

            if y_size > 1:
                across(n, z_at).wait_send()
        return carry

    lax.fori_loop(0, z_size, sent_z, 0)

    def sent_chip(chip_at, carry):
        z_at = chip_at // y_size
        y_at = lax.rem(chip_at, y_size)
        if shared:

            @pl.when(chip_at != chip)
            def _():
                for n in range(swapped):
                    over(n, z_at, y_at).wait_send()

        for quarter in range(PIECES):
            beside(quarter, z_at, y_at).wait_send()
        return carry

    lax.fori_loop(0, chips, sent_chip, 0)

    def sent_rows(step):
        row_copy(step).wait_send()
        part_copy(bias_parts, bias_send, bias_recv, step, False).wait_send()

    each_peer(sent_rows)
    each_peer(
        lambda step: part_copy(hidden_parts, hidden_send, hidden_recv, step, True).wait_recv()
    )
    hidden_ref[...] = (jnp.sum(hidden_parts[...], axis=0) * scale).reshape(hidden_ref.shape)
    each_peer(
        lambda step: part_copy(hidden_parts, hidden_send, hidden_recv, step, False).wait_send()
    )


def per_device(grp_size, cotangent, vis_count, vis_pos, patch_owner, pre_act, proj_weight):
    ctx_size = lax.axis_size("ctx")
    tok_rows, row_width = cotangent.shape
    per_peer = tok_rows // ctx_size
    owned, hidden = pre_act.shape
    units, _ = proj_weight.shape
    chips = ctx_size // 2
    y_size = 2 if chips == 8 else 1
    z_size = chips // y_size
    swapped = SWAPPED if grp_size % 2 == 0 else 0
    own_pieces = PIECES - swapped
    width = row_width // PIECES

    vmem = pl.BlockSpec(memory_space=pltpu.VMEM)
    dma = pltpu.SemaphoreType.DMA
    pre_act_grad, hidden_sum, out_sum = pl.pallas_call(
        functools.partial(
            kernel, grp_size, ctx_size, z_size, y_size, 1.0 / math.sqrt(owned * ctx_size)
        ),
        out_shape=(
            jax.ShapeDtypeStruct((owned, hidden), jnp.bfloat16),
            jax.ShapeDtypeStruct((hidden,), jnp.float32),
            jax.ShapeDtypeStruct((row_width,), jnp.float32),
        ),
        in_specs=[vmem] * 3 + [pl.BlockSpec(memory_space=pl.ANY)] * 3,
        out_specs=(vmem, vmem, vmem),
        scratch_shapes=[
            pltpu.VMEM((tok_rows, row_width), jnp.bfloat16),
            pltpu.VMEM((owned, hidden), jnp.bfloat16),
            pltpu.VMEM((PIECES, ctx_size, units, width), jnp.bfloat16),
            pltpu.VMEM((ctx_size, per_peer, row_width), jnp.bfloat16),
            pltpu.VMEM((ctx_size, per_peer, row_width), jnp.bfloat16),
            pltpu.VMEM((owned, row_width), jnp.bfloat16),
            pltpu.VMEM((ctx_size, 1, row_width), jnp.float32),
            pltpu.VMEM((ctx_size, 1, hidden), jnp.float32),
            dma((PIECES + 2,)),
            dma((PIECES, ctx_size)),
            dma((2, own_pieces, z_size)),
            dma((own_pieces, z_size)),
            dma((max(swapped, 1), chips)),
            dma((PIECES, chips)),
            dma((ctx_size,)),
            dma((ctx_size,)),
            dma((ctx_size,)),
            dma((ctx_size,)),
            dma((ctx_size,)),
            dma((ctx_size,)),
        ],
        compiler_params=pltpu.CompilerParams(
            collective_id=0, has_side_effects=True, vmem_limit_bytes=56 * 1024 * 1024
        ),
        cost_estimate=pl.CostEstimate(
            flops=2 * owned * hidden * row_width,
            bytes_accessed=8 * owned * row_width,
            transcendentals=owned * hidden,
        ),
    )(
        vis_count,
        vis_pos,
        patch_owner,
        cotangent,
        pre_act,
        proj_weight,
    )
    return (pre_act_grad, hidden_sum, out_sum)


def solution(mesh):
    return jax.shard_map(
        functools.partial(per_device, mesh.shape["grp"]),
        mesh=mesh,
        in_specs=(
            P(("grp", "ctx"), None),
            P("grp"),
            P(("grp", "ctx")),
            P("grp"),
            P(("grp", "ctx"), None),
            P("ctx", None),
        ),
        out_specs=(P(("grp", "ctx"), None), P("grp"), P("grp")),
        check_vma=False,
    )
```

```python
import functools
import math

import jax
import jax.numpy as jnp
from jax import lax
from jax.experimental import pallas as pl
from jax.experimental.pallas import tpu as pltpu
from jax.sharding import PartitionSpec as P

PIECES = 8
SWAPPED = 4
ROW_FROM = 1
MESH = pl.DeviceIdType.MESH


def gelu_slope(x):
    k = math.sqrt(2.0 / math.pi)
    square = x * x
    t = jnp.tanh(x * (k + (k * 0.044715) * square))
    return 0.5 * (1.0 + t) + (0.5 * x) * ((1.0 - t * t) * (k + (3.0 * 0.044715 * k) * square))


def kernel(
    grp_size,
    ctx_size,
    z_size,
    y_size,
    scale,
    count_ref,
    pos_ref,
    owner_ref,
    cot_hbm,
    pre_hbm,
    w_hbm,
    out_ref,
    hidden_ref,
    bias_ref,
    cot_ref,
    pre_ref,
    w_all,
    outgoing,
    received,
    rows,
    bias_parts,
    hidden_parts,
    load_sem,
    w_recv,
    z_send,
    y_send,
    x_send,
    s_send,
    row_send,
    row_recv,
    bias_send,
    bias_recv,
    hidden_send,
    hidden_recv,
):
    grp = lax.axis_index("grp")
    me = lax.axis_index("ctx")
    core = lax.rem(me, 2)
    chip = me // 2
    y = lax.rem(chip, y_size)
    z = chip // y_size
    chips = z_size * y_size
    shared = grp_size % 2 == 0
    swapped = SWAPPED if shared else 0
    own_pieces = PIECES - swapped
    half = lax.rem(grp, 2) if shared else 0
    width = w_all.shape[3]
    tok_rows = cot_ref.shape[0]
    per_peer = tok_rows // ctx_size

    def own_piece(n):
        return half * swapped + n if n < swapped else swapped + n

    def other_piece(n):
        return (1 - half) * swapped + n

    def index(z_at, y_at, core_at):
        return (z_at * y_size + y_at) * 2 + core_at

    sibling = {"ctx": index(z, y, 1 - core)}
    y_peer = {"ctx": index(z, y_size - 1 - y, core)}
    z_up = {"ctx": index(jnp.minimum(z + 1, z_size - 1), y, core)}
    z_down = {"ctx": index(jnp.maximum(z - 1, 0), y, core)}
    x_peer = {"grp": grp + 1 - 2 * lax.rem(grp, 2)}

    own_shard = [
        pltpu.make_async_copy(
            w_hbm.at[:, pl.ds(at * width, width)], w_all.at[at, me], load_sem.at[at]
        )
        for at in range(PIECES)
    ]
    for load in own_shard:
        load.start()
    barrier = pltpu.get_barrier_semaphore()

    def greet(step, carry):
        pl.semaphore_signal(
            barrier, inc=1, device_id={"ctx": lax.rem(me + step, ctx_size)}, device_id_type=MESH
        )
        return carry

    lax.fori_loop(1, ctx_size, greet, 0)
    if shared:
        pl.semaphore_signal(barrier, inc=1, device_id=x_peer, device_id_type=MESH)
    loads = [pltpu.make_async_copy(cot_hbm, cot_ref, load_sem.at[PIECES])]
    loads += [pltpu.make_async_copy(pre_hbm, pre_ref, load_sem.at[PIECES + 1])]
    for load in loads:
        load.start()
    for load in own_shard:
        load.wait()
    pl.semaphore_wait(barrier, ctx_size if shared else ctx_size - 1)

    def piece(quarter, origin, sem, device):
        return pltpu.make_async_remote_copy(
            src_ref=w_all.at[quarter, origin],
            dst_ref=w_all.at[quarter, origin],
            send_sem=sem,
            recv_sem=w_recv.at[quarter, origin],
            device_id=device,
            device_id_type=MESH,
        )

    def up(n, z_at):
        return piece(own_piece(n), index(z_at, y, core), z_send.at[0, n, z_at], z_up)

    def down(n, z_at):
        return piece(own_piece(n), index(z_at, y, core), z_send.at[1, n, z_at], z_down)

    def across(n, z_at):
        return piece(own_piece(n), index(z_at, y, core), y_send.at[n, z_at], y_peer)

    def over(n, z_at, y_at):
        return piece(
            own_piece(n),
            index(z_at, y_at, core),
            x_send.at[n, z_at * y_size + y_at],
            x_peer,
        )

    def beside(quarter, z_at, y_at):
        return piece(
            quarter, index(z_at, y_at, core), s_send.at[quarter, z_at * y_size + y_at], sibling
        )

    def arrived(quarter, origin):
        piece(quarter, origin, s_send.at[0, 0], sibling).wait_recv()

    for n in range(own_pieces):

        @pl.when(z < z_size - 1)
        def _():
            up(n, z).start()

        @pl.when(z > 0)
        def _():
            down(n, z).start()

        if y_size > 1:
            across(n, z).start()
    for quarter in range(PIECES):
        beside(quarter, z, y).start()

    blocks = lax.div(count_ref[...].reshape(1, ctx_size), ctx_size).astype(jnp.float32)
    peers = lax.broadcasted_iota(jnp.int32, (1, ctx_size), 1)
    my_first = jnp.sum(jnp.where(peers < me, blocks, 0.0), axis=1, keepdims=True)
    my_blocks = jnp.sum(jnp.where(peers == me, blocks, 0.0), axis=1, keepdims=True)
    token = lax.broadcasted_iota(jnp.int32, (1, tok_rows), 1)
    start = (my_first * ctx_size).astype(jnp.int32)
    chunk = math.gcd(owner_ref.shape[0], 1024)
    offset = lax.broadcasted_iota(jnp.int32, (chunk, tok_rows), 0) - lax.broadcasted_iota(
        jnp.int32, (chunk, tok_rows), 1
    )
    owner = jnp.zeros((8, tok_rows), jnp.float32)
    for at in range(0, owner_ref.shape[0], chunk):
        part = owner_ref[at : at + chunk].reshape(1, chunk).astype(jnp.float32)
        part = jnp.broadcast_to(part, (8, chunk)).astype(jnp.bfloat16)
        hit = jnp.where(offset == start - at, 1.0, 0.0).astype(jnp.bfloat16)
        owner += jnp.dot(part, hit, preferred_element_type=jnp.float32)
    nth_block = lax.div(token, ctx_size)
    target = jnp.where(
        nth_block.astype(jnp.float32) < my_blocks,
        owner[0:1].astype(jnp.int32) * per_peer + nth_block,
        -1,
    )

    source = lax.div(token, per_peer)
    nth = (token - source * per_peer).astype(jnp.float32)
    peer_rows = lax.broadcasted_iota(jnp.int32, (ctx_size, tok_rows), 0)
    counts = jnp.broadcast_to(blocks, (8, ctx_size)).astype(jnp.bfloat16)
    before = jnp.where(peer_rows < source, 1.0, 0.0).astype(jnp.bfloat16)
    equal = jnp.where(peer_rows == source, 1.0, 0.0).astype(jnp.bfloat16)
    first = jnp.dot(counts, before, preferred_element_type=jnp.float32)[0:1]
    held = jnp.dot(counts, equal, preferred_element_type=jnp.float32)[0:1]
    slot = jnp.where(nth < held, first + nth, -1.0).astype(jnp.int32)

    for load in loads:
        load.wait()
    slots = lax.broadcasted_iota(jnp.int32, (tok_rows, tok_rows), 0)
    to_slot = jnp.where(slots == target, 1.0, 0.0).astype(jnp.bfloat16)
    to_pos = jnp.where(slots == pos_ref[...].reshape(1, tok_rows), 1.0, 0.0).astype(jnp.bfloat16)
    pick = lax.dot_general(
        to_slot, to_pos, (((1,), (1,)), ((), ())), preferred_element_type=jnp.float32
    ).astype(jnp.bfloat16)
    step_width = 512
    for at in range(0, cot_ref.shape[1], step_width):
        cols = slice(at, at + step_width)
        packed = jnp.dot(pick, cot_ref[:, cols], preferred_element_type=jnp.float32)
        outgoing[:, :, cols] = packed.astype(jnp.bfloat16).reshape(ctx_size, per_peer, step_width)
        bias_parts[me, :, cols] = jnp.sum(packed, axis=0, keepdims=True)

    def row_copy(step):
        peer = lax.rem(me + step, ctx_size)
        return pltpu.make_async_remote_copy(
            src_ref=outgoing.at[peer],
            dst_ref=received.at[me],
            send_sem=row_send.at[peer],
            recv_sem=row_recv.at[me],
            device_id={"ctx": peer},
            device_id_type=MESH,
        )

    def row_arrival(step):
        peer = lax.rem(me + step, ctx_size)
        return pltpu.make_async_remote_copy(
            src_ref=outgoing.at[peer],
            dst_ref=received.at[peer],
            send_sem=row_send.at[peer],
            recv_sem=row_recv.at[peer],
            device_id={"ctx": peer},
            device_id_type=MESH,
        )

    def part_copy(parts, send, recv, step, arrival):
        peer = lax.rem(me + step, ctx_size)
        slot = peer if arrival else me
        return pltpu.make_async_remote_copy(
            src_ref=parts.at[slot],
            dst_ref=parts.at[slot],
            send_sem=send.at[peer],
            recv_sem=recv.at[slot],
            device_id={"ctx": peer},
            device_id_type=MESH,
        )

    def each_peer(body):
        def run(step, carry):
            body(step)
            return carry

        lax.fori_loop(1, ctx_size, run, 0)

    def send_rows(step):
        row_copy(step).start()
        part_copy(bias_parts, bias_send, bias_recv, step, False).start()

    received[me] = outgoing[me]
    turns = own_pieces * (z_size + 1)
    batch = max(-(-(ctx_size - 1) // (turns // 1)), 1)

    def send_batch(t, n):
        if n % 1 == 0:
            first_step = ((t - 1) * -(-own_pieces // 1) + n // 1) * batch + 1
            for at in range(batch):

                @pl.when(first_step + at < ctx_size)
                def _():
                    send_rows(lax.rem((first_step + at) * 7, ctx_size))

    def pass_z(n, z_at, rising):
        arrived(own_piece(n), index(z_at, y, core))
        if rising:

            @pl.when(z < z_size - 1)
            def _():
                up(n, z_at).start()

        else:

            @pl.when(z > 0)
            def _():
                down(n, z_at).start()

        if y_size > 1:
            across(n, z_at).start()
        if n < swapped:
            over(n, z_at, y).start()
        beside(own_piece(n), z_at, y).start()

    def pass_y(n, z_at):
        arrived(own_piece(n), index(z_at, y_size - 1 - y, core))
        if n < swapped:
            over(n, z_at, y_size - 1 - y).start()
        beside(own_piece(n), z_at, y_size - 1 - y).start()

    def pass_x(n, z_at, y_at):
        arrived(other_piece(n), index(z_at, y_at, core))
        beside(other_piece(n), z_at, y_at).start()

    def at_distance(d, body):
        @pl.when((d >= 0) & (z - d >= 0))
        def _():
            body(z - d, True)

        @pl.when((d > 0) & (z + d < z_size))
        def _():
            body(z + d, False)

    def forward_piece(n, t):
        @pl.when(t < z_size)
        def _():
            at_distance(t, lambda z_at, rising: pass_z(n, z_at, rising))

        if y_size > 1:

            @pl.when(t - 1 < z_size)
            def _():
                at_distance(t - 1, lambda z_at, rising: pass_y(n, z_at))

        if n < swapped:

            def both(z_at, rising):
                @pl.when(z_at != z)
                def _():
                    pass_x(n, z_at, y)

                if y_size > 1:
                    pass_x(n, z_at, y_size - 1 - y)

            @pl.when(t - 2 < z_size)
            def _():
                at_distance(t - 2, both)

    def forward(t, carry):
        for n in range(own_pieces):
            send_batch(t, n)
            forward_piece(n, t)
        return carry

    lax.fori_loop(1, z_size + 2, forward, 0)

    each_peer(lambda step: row_arrival(step).wait_recv())
    owned = rows.shape[0]
    slot_ids = lax.broadcasted_iota(jnp.int32, (owned, tok_rows), 0)
    place = jnp.where(slot_ids == slot, 1.0, 0.0).astype(jnp.bfloat16)
    for at in range(0, cot_ref.shape[1], step_width):
        cols = slice(at, at + step_width)
        landed = received[:, :, cols].reshape(tok_rows, step_width)
        rows[:, cols] = jnp.dot(place, landed, preferred_element_type=jnp.float32).astype(
            jnp.bfloat16
        )

    def side(chip_at, carry):
        for quarter in range(PIECES):
            arrived(quarter, chip_at * 2 + 1 - core)
        return carry

    lax.fori_loop(0, chips, side, 0)

    group = ctx_size // 2
    units = group * w_all.shape[2]

    def multiply(at, carry):
        total = jnp.zeros((owned, units), jnp.float32)
        for quarter in range(PIECES):
            block = w_all[quarter, pl.ds(at * group, group)].reshape(units, width)
            total += lax.dot_general(
                rows[:, quarter * width : (quarter + 1) * width],
                block,
                (((1,), (1,)), ((), ())),
                preferred_element_type=jnp.float32,
            )
        cols = pl.ds(pl.multiple_of(at * units, 128), units)
        grad = total * gelu_slope(pre_ref[:, cols].astype(jnp.float32))
        out_ref[:, cols] = grad.astype(jnp.bfloat16)
        hidden_parts[me, :, cols] = jnp.sum(grad, axis=0, keepdims=True)
        return carry

    lax.fori_loop(0, 2, multiply, 0)
    each_peer(
        lambda step: part_copy(hidden_parts, hidden_send, hidden_recv, step, False).start()
    )

    each_peer(lambda step: part_copy(bias_parts, bias_send, bias_recv, step, True).wait_recv())
    bias_ref[...] = (jnp.sum(bias_parts[...], axis=0) * scale).reshape(bias_ref.shape)

    def sent_z(z_at, carry):
        for n in range(own_pieces):

            @pl.when((z < z_size - 1) & (z_at <= z))
            def _():
                up(n, z_at).wait_send()

            @pl.when((z > 0) & (z_at >= z))
            def _():
                down(n, z_at).wait_send()

            if y_size > 1:
                across(n, z_at).wait_send()
        return carry

    lax.fori_loop(0, z_size, sent_z, 0)

    def sent_chip(chip_at, carry):
        z_at = chip_at // y_size
        y_at = lax.rem(chip_at, y_size)
        if shared:

            @pl.when(chip_at != chip)
            def _():
                for n in range(swapped):
                    over(n, z_at, y_at).wait_send()

        for quarter in range(PIECES):
            beside(quarter, z_at, y_at).wait_send()
        return carry

    lax.fori_loop(0, chips, sent_chip, 0)

    def sent_rows(step):
        row_copy(step).wait_send()
        part_copy(bias_parts, bias_send, bias_recv, step, False).wait_send()

    each_peer(sent_rows)
    each_peer(
        lambda step: part_copy(hidden_parts, hidden_send, hidden_recv, step, True).wait_recv()
    )
    hidden_ref[...] = (jnp.sum(hidden_parts[...], axis=0) * scale).reshape(hidden_ref.shape)
    each_peer(
        lambda step: part_copy(hidden_parts, hidden_send, hidden_recv, step, False).wait_send()
    )


def per_device(grp_size, cotangent, vis_count, vis_pos, patch_owner, pre_act, proj_weight):
    ctx_size = lax.axis_size("ctx")
    tok_rows, row_width = cotangent.shape
    per_peer = tok_rows // ctx_size
    owned, hidden = pre_act.shape
    units, _ = proj_weight.shape
    chips = ctx_size // 2
    y_size = 2 if chips == 8 else 1
    z_size = chips // y_size
    swapped = SWAPPED if grp_size % 2 == 0 else 0
    own_pieces = PIECES - swapped
    width = row_width // PIECES

    vmem = pl.BlockSpec(memory_space=pltpu.VMEM)
    dma = pltpu.SemaphoreType.DMA
    pre_act_grad, hidden_sum, out_sum = pl.pallas_call(
        functools.partial(
            kernel, grp_size, ctx_size, z_size, y_size, 1.0 / math.sqrt(owned * ctx_size)
        ),
        out_shape=(
            jax.ShapeDtypeStruct((owned, hidden), jnp.bfloat16),
            jax.ShapeDtypeStruct((hidden,), jnp.float32),
            jax.ShapeDtypeStruct((row_width,), jnp.float32),
        ),
        in_specs=[vmem] * 3 + [pl.BlockSpec(memory_space=pl.ANY)] * 3,
        out_specs=(vmem, vmem, vmem),
        scratch_shapes=[
            pltpu.VMEM((tok_rows, row_width), jnp.bfloat16),
            pltpu.VMEM((owned, hidden), jnp.bfloat16),
            pltpu.VMEM((PIECES, ctx_size, units, width), jnp.bfloat16),
            pltpu.VMEM((ctx_size, per_peer, row_width), jnp.bfloat16),
            pltpu.VMEM((ctx_size, per_peer, row_width), jnp.bfloat16),
            pltpu.VMEM((owned, row_width), jnp.bfloat16),
            pltpu.VMEM((ctx_size, 1, row_width), jnp.float32),
            pltpu.VMEM((ctx_size, 1, hidden), jnp.float32),
            dma((PIECES + 2,)),
            dma((PIECES, ctx_size)),
            dma((2, own_pieces, z_size)),
            dma((own_pieces, z_size)),
            dma((max(swapped, 1), chips)),
            dma((PIECES, chips)),
            dma((ctx_size,)),
            dma((ctx_size,)),
            dma((ctx_size,)),
            dma((ctx_size,)),
            dma((ctx_size,)),
            dma((ctx_size,)),
        ],
        compiler_params=pltpu.CompilerParams(
            collective_id=0, has_side_effects=True, vmem_limit_bytes=56 * 1024 * 1024
        ),
        cost_estimate=pl.CostEstimate(
            flops=2 * owned * hidden * row_width,
            bytes_accessed=8 * owned * row_width,
            transcendentals=owned * hidden,
        ),
    )(
        vis_count,
        vis_pos,
        patch_owner,
        cotangent,
        pre_act,
        proj_weight,
    )
    return (pre_act_grad, hidden_sum, out_sum)


def solution(mesh):
    return jax.shard_map(
        functools.partial(per_device, mesh.shape["grp"]),
        mesh=mesh,
        in_specs=(
            P(("grp", "ctx"), None),
            P("grp"),
            P(("grp", "ctx")),
            P("grp"),
            P(("grp", "ctx"), None),
            P("ctx", None),
        ),
        out_specs=(P(("grp", "ctx"), None), P("grp"), P("grp")),
        check_vma=False,
    )
```
